256 devices in a mesh: tile: 32 (over z_hi, x, y), day: 8 (over z_lo, core).
Axes of the slice: x: 4, y: 4, z: 8 (z_hi: 2, z_lo: 4; z = z_hi * 4 + z_lo), core: 2. Of those that a mesh axis runs over, the one named last changes fastest.
Arguments:
- spectra: bfloat16 [8192, 24, 6, 1024], P('tile', 'day'), may hold values from -6 to 6
- send_list: int32 [4096], P('tile'), may hold values from 0 to 255
- pair_first: int32 [32768], P('tile'), may hold values from 0 to 255
- pair_second: int32 [32768], P('tile'), may hold values from 0 to 383, as said below
Outputs:
- stacked_corr: float32 [32768, 1001], P(('tile', 'day'))
The draws below stay inside these ranges and needn't reach their ends.
Inputs may be any that keep to these rules, and one draw needn't show every extreme that they name: `pair_second`: slots 0 to 255 of the table are the tile's own stations, the next 64 come from the tile below and the last 64 from the tile above; the first tile's pairs never use slots from below, the last tile's never those from above.
All inputs are finite; a program needn't handle non-finite values.
Results may differ from the reference program's by a relative error of at most 0.0003.
Values may be sent and summed in bfloat16 or wider, within the bound.
No kernel may reach another device: no remote copies, remote signals or barrier semaphores. Data moves between devices by JAX's collectives and lax.ppermute only.
A program may use at most 128 MiB of HBM per device.

```python
import math
import jax
import jax.numpy as jnp
from jax import lax

NF = 512
HALF_LAG = 500
SEGS = 6
STA_TILE = 256
HALO = 64
PAIR_TILE = 1024
DAYS = 24
STATIONS = 8192
PAIRS = 32768
N_TILE = 32


def draw_pair_second(key, part):
    key = jax.random.fold_in(key, 11)
    position = jnp.arange(PAIRS, dtype=jnp.int32)
    owner = position // PAIR_TILE
    slots = jax.random.randint(key, (PAIRS,), 0, STA_TILE + 2 * HALO, dtype=jnp.int32)
    from_below = (slots >= STA_TILE) & (slots < STA_TILE + HALO)
    from_above = slots >= STA_TILE + HALO
    slots = jnp.where((owner == 0) & from_below, slots + HALO, slots)
    slots = jnp.where((owner == N_TILE - 1) & from_above, slots - HALO, slots)
    return slots


def plant(entries, own_key, least, top_value):
    longest = entries.shape.index(max(entries.shape))
    spots = []
    for shift in (0, 1):
        where = [jax.random.randint(jax.random.fold_in(own_key, axis), (), 0, length) for axis, length in enumerate(entries.shape)]
        where[longest] = (where[longest] + shift) % entries.shape[longest]
        spots.append(tuple(where))
    return entries.at[spots[0]].set(least).at[spots[1]].set(top_value)


def block_scale(key, extent, pieces, low, high):
    loudness = 1.0
    for dim, shards_of in pieces:
        draws = jax.random.uniform(jax.random.fold_in(jax.random.fold_in(key, 6), dim), (shards_of,), jnp.float32, low / len(pieces), high / len(pieces))
        loudness = loudness * jnp.repeat(jnp.exp(draws), extent[dim] // shards_of).reshape((-1,) + (1,) * (len(extent) - 1 - dim))
    return loudness


def noise(key, shape, deviation, most, cuts=(), kind=jnp.bfloat16):
    array = deviation * jax.random.normal(key, shape, jnp.float32)
    if cuts:
        array = array * block_scale(key, shape, cuts, -0.22, 0.18)
    return jnp.clip(array, -most, most).astype(kind)


def setup_inputs(seed: int = 0) -> dict:
    splits = jax.random.split(jax.random.key(seed), 5)
    spectra = noise(splits[0], (STATIONS, DAYS, SEGS, 2 * NF), 1.0, 6.0, ((0, 32), (1, 8)))
    send_list = plant(jax.random.randint(splits[1], (N_TILE * 2 * HALO,), 0, STA_TILE), jax.random.fold_in(splits[1], 1), 0, STA_TILE - 1).astype(jnp.int32)
    pair_first = plant(jax.random.randint(splits[2], (PAIRS,), 0, STA_TILE), jax.random.fold_in(splits[2], 1), 0, STA_TILE - 1).astype(jnp.int32)
    pair_second = draw_pair_second(jax.random.fold_in(splits[4], 71), 0)
    return {"spectra": spectra, "send_list": send_list, "pair_first": pair_first, "pair_second": pair_second}


def lag_table(freq_bins, half_lag):
    column = jnp.arange(freq_bins, dtype=jnp.int32)[:, None]
    shifts = jnp.arange(2 * half_lag + 1, dtype=jnp.int32)[None, :] - half_lag
    phases = column * shifts % (2 * freq_bins)
    angles = phases.astype(jnp.float32) * (math.pi / freq_bins)
    return jnp.concatenate([jnp.cos(angles), -jnp.sin(angles)], axis=0)

def cross_rows(first_rows, second_rows, freq_bins):
    first_real = first_rows[..., :freq_bins].astype(jnp.float32)
    first_imag = first_rows[..., freq_bins:].astype(jnp.float32)
    second_real = second_rows[..., :freq_bins].astype(jnp.float32)
    second_imag = second_rows[..., freq_bins:].astype(jnp.float32)
    real_part = lax.optimization_barrier(jnp.sum(first_real * second_real + first_imag * second_imag, axis=(1, 2)))
    imag_part = lax.optimization_barrier(jnp.sum(first_imag * second_real - first_real * second_imag, axis=(1, 2)))
    return jnp.concatenate([real_part, imag_part], axis=-1)

def pair_spectra(own, station_table, first_ids, second_ids):
    count = first_ids.shape[0]
    width = min(count, 128)
    freq_bins = own.shape[-1] // 2
    first_blocks = first_ids.reshape(count // width, width)
    second_blocks = second_ids.reshape(count // width, width)

    def one_block(ids):
        return cross_rows(own[ids[0]], station_table[ids[1]], freq_bins)
    result = lax.map(one_block, (first_blocks, second_blocks))
    return result.reshape(count, 2 * freq_bins)

def reference(spectra, send_list, pair_first, pair_second):
    tiles = spectra.reshape(N_TILE, STA_TILE, DAYS, SEGS, 2 * NF)
    sends = send_list.reshape(N_TILE, 2 * HALO)
    firsts = pair_first.reshape(N_TILE, PAIR_TILE)
    seconds = pair_second.reshape(N_TILE, PAIR_TILE)
    weights = lag_table(NF, HALF_LAG)
    scale = 1.0 / math.sqrt(2 * NF * SEGS * DAYS)

    def one_tile(index):
        own = tiles[index]
        below = jnp.maximum(index - 1, 0)
        above = jnp.minimum(index + 1, N_TILE - 1)
        from_below = tiles[below][sends[below][HALO:]]
        from_above = tiles[above][sends[above][:HALO]]
        from_below = jnp.where(index > 0, from_below, jnp.zeros_like(from_below))
        from_above = jnp.where(index < N_TILE - 1, from_above, jnp.zeros_like(from_above))
        station_table = jnp.concatenate([own, from_below, from_above], axis=0)
        cross = pair_spectra(own, station_table, firsts[index], seconds[index])
        return jnp.dot(cross, weights, precision=lax.Precision.HIGHEST, preferred_element_type=jnp.float32) * scale
    result = lax.map(one_tile, jnp.arange(N_TILE, dtype=jnp.int32))
    return result.reshape(N_TILE * PAIR_TILE, 2 * HALF_LAG + 1)
```

```python
import functools

import jax
import jax.numpy as jnp
import numpy as np
from jax import lax
from jax.experimental import pallas as pl
from jax.experimental.pallas import tpu as pltpu
from jax.sharding import PartitionSpec as P

HALF_LAG = 500
LANES = 128
CHUNKS = ((0, 1), (2, 3))
PAIR_BLOCK = 256
SEG_STEP = 6
VMEM = 60 << 20
SCALE_ROWS = 16
TOP = 32000.0


def one_hot(ids, width, base):
    slots = lax.broadcasted_iota(jnp.int32, (ids.shape[0], width), 1) + base
    return (ids == slots).astype(jnp.float32).astype(jnp.bfloat16)


def anywhere():
    return pl.BlockSpec(memory_space=pl.ANY)


def scalars():
    return pl.BlockSpec(memory_space=pltpu.SMEM)


def params():
    return pltpu.CompilerParams(vmem_limit_bytes=VMEM)


def border_kernel(flag_ref, send_ref, real_ref, imag_ref, below_ref, above_ref, next_ref, pick_ref):
    next_ref[0] = flag_ref[0]

    @pl.when((pl.program_id(0) == 0) & (pl.program_id(1) == 0))
    def _():
        pick_ref[...] = one_hot(send_ref[...], pick_ref.shape[1], 0)

    half = below_ref.shape[1]
    step = real_ref.shape[0]
    for seg in range(step):
        rows = jnp.concatenate([real_ref[seg], imag_ref[seg]], axis=1)
        lent = jnp.dot(pick_ref[...], rows, preferred_element_type=jnp.float32)
        lent = lent.astype(jnp.bfloat16)
        below_ref[seg] = lent[:half]
        above_ref[seg] = lent[half:]


def lent_rows(flags, spectra, send_list, chunk):
    groups, stations, width = spectra.shape
    count = send_list.shape[0]
    half = count // 2
    first, blocks = chunk[0], len(chunk)
    offset = width // 2 // LANES
    step = 9
    lanes = 2 * LANES * blocks
    out = jax.ShapeDtypeStruct((groups, half, lanes), jnp.bfloat16)
    out_spec = pl.BlockSpec((step, half, 2 * LANES), lambda j, g: (g, 0, j))
    return pl.pallas_call(
        border_kernel,
        grid=(blocks, groups // step),
        in_specs=[
            scalars(),
            pl.BlockSpec((count, 1), lambda j, g: (0, 0)),
            pl.BlockSpec((step, stations, LANES), lambda j, g: (g, 0, first + j)),
            pl.BlockSpec((step, stations, LANES), lambda j, g: (g, 0, first + j + offset)),
        ],
        out_specs=[out_spec, out_spec, scalars()],
        out_shape=[out, out, jax.ShapeDtypeStruct((1,), jnp.int32)],
        scratch_shapes=[pltpu.VMEM((count, stations), jnp.bfloat16)],
        compiler_params=params(),
        cost_estimate=pl.CostEstimate(
            flops=2 * count * stations * groups * lanes,
            bytes_accessed=groups * (stations + count) * lanes * 2,
            transcendentals=0,
        ),
    )(flags, send_list.reshape(count, 1), spectra, spectra)


def cross_kernel(
    flag_ref, first_ref, second_ref, real_ref, imag_ref, below_ref, above_ref, relay_ref, token_ref,
    send_ref, keep_ref, own_ref, halo_ref, border_ref,
):
    stations = real_ref.shape[1]
    lent = below_ref.shape[1]
    blocks = own_ref.shape[0]
    size = halo_ref.shape[1]
    groups = real_ref.shape[0]
    turn = pl.program_id(1)

    @pl.when((pl.program_id(0) == 0) & (turn == 0))
    def _():
        for block in range(blocks):
            rows = slice(block * size, (block + 1) * size)
            own_ref[block, :size] = one_hot(first_ref[rows], stations, 0)
            own_ref[block, size:] = one_hot(second_ref[rows], stations, 0)
            halo_ref[block] = one_hot(second_ref[rows], 2 * lent, stations)

    @pl.when(turn == 0)
    def _():
        send_ref[...] = jnp.zeros_like(send_ref)
        keep_ref[...] = jnp.zeros_like(keep_ref)

    border_ref[:, :lent] = below_ref[...]
    border_ref[:, lent:] = above_ref[...]

    @pl.when(flag_ref[0] == 1)
    def _():
        border_ref[:, :lent] = relay_ref[...]

    @pl.when(flag_ref[0] == 2)
    def _():
        border_ref[:, lent:] = relay_ref[...]

    for block in range(blocks):
        out_ref = (send_ref, keep_ref)[block // (blocks // 2)]
        start = block % (blocks // 2) * size
        rows = slice(start, start + size)
        real = out_ref[rows, :LANES]
        imag = out_ref[rows, LANES:]
        for seg in range(groups):
            table = jnp.concatenate([real_ref[seg], imag_ref[seg]], axis=1)
            both = jnp.dot(own_ref[block], table, preferred_element_type=jnp.float32)
            a = both[:size]
            b = both[size:] + jnp.dot(halo_ref[block], border_ref[seg], preferred_element_type=jnp.float32)
            ar, ai, br, bi = a[:, :LANES], a[:, LANES:], b[:, :LANES], b[:, LANES:]
            real = real + (ar * br + ai * bi)
            imag = imag + (ai * br - ar * bi)
        out_ref[rows, :LANES] = real
        out_ref[rows, LANES:] = imag


def pair_cross(flags, first_ids, second_ids, spectra, halo, chunk, token):
    below, above, relay = halo
    groups, stations, width = spectra.shape
    pairs = first_ids.shape[0]
    lent = below.shape[1]
    offset = width // 2 // LANES
    blocks = pairs // PAIR_BLOCK
    first, parts = chunk[0], len(chunk)
    ids_spec = pl.BlockSpec((pairs, 1), lambda j, g: (0, 0))
    halo_spec = pl.BlockSpec((SEG_STEP, lent, 2 * LANES), lambda j, g: (g, 0, j))

    out = jax.ShapeDtypeStruct((pairs // 2, 2 * LANES * parts), jnp.float32)
    return pl.pallas_call(
        cross_kernel,
        grid=(parts, groups // SEG_STEP),
        in_specs=[
            scalars(),
            ids_spec,
            ids_spec,
            pl.BlockSpec((SEG_STEP, stations, LANES), lambda j, g: (g, 0, first + j)),
            pl.BlockSpec((SEG_STEP, stations, LANES), lambda j, g: (g, 0, first + j + offset)),
            halo_spec,
            halo_spec,
            halo_spec,
            anywhere(),
        ],
        out_specs=[pl.BlockSpec((pairs // 2, 2 * LANES), lambda j, g: (0, j))] * 2,
        out_shape=[out, out],
        scratch_shapes=[
            pltpu.VMEM((blocks, 2 * PAIR_BLOCK, stations), jnp.bfloat16),
            pltpu.VMEM((blocks, PAIR_BLOCK, 2 * lent), jnp.bfloat16),
            pltpu.VMEM((SEG_STEP, 2 * lent, 2 * LANES), jnp.bfloat16),
        ],
        compiler_params=params(),
        cost_estimate=pl.CostEstimate(
            flops=2 * pairs * (2 * stations + 2 * lent) * groups * 2 * LANES * parts,
            bytes_accessed=groups * (stations + 2 * lent) * 2 * LANES * 2 * parts,
            transcendentals=0,
        ),
    )(flags, first_ids, second_ids, spectra, spectra, below, above, relay, token)


def pack_kernel(keep_ref, other_ref, token_ref, own_ref, *out_refs):
    kept = own_ref.shape[0]
    own_ref[...] = keep_ref[:kept] + other_ref[:kept]
    for k, out_ref in enumerate(out_refs, 1):
        rows = slice(k * kept, (k + 1) * kept)
        total = keep_ref[rows] + other_ref[rows]
        peak = jnp.max(jnp.abs(total), axis=0, keepdims=True)
        power = jnp.ceil(jnp.log2(jnp.maximum(peak, 1e-36) * 1.0001))
        scaled = jnp.round(total * jnp.exp2(-power) * TOP)
        out_ref[:kept] = scaled.astype(jnp.int32).astype(jnp.int16)
        powers = jnp.broadcast_to(power, (SCALE_ROWS, power.shape[1]))
        out_ref[kept:] = powers.astype(jnp.int32).astype(jnp.int16)


def pack(keep, other, token, parts):
    rows, lanes = keep.shape
    kept = rows // parts
    coded = jax.ShapeDtypeStruct((kept + SCALE_ROWS, lanes), jnp.int16)
    whole = pl.BlockSpec(memory_space=pltpu.VMEM)
    return pl.pallas_call(
        pack_kernel,
        in_specs=[whole, whole, anywhere()],
        out_specs=[whole] * parts,
        out_shape=[jax.ShapeDtypeStruct((kept, lanes), jnp.float32)] + [coded] * (parts - 1),
        compiler_params=params(),
    )(keep, other, token)


def unpack(ref, kept):
    power = ref[kept:].astype(jnp.int32).astype(jnp.float32)[:1]
    return ref[:kept].astype(jnp.int32).astype(jnp.float32) * (1.0 / TOP) * jnp.exp2(power)


def lag_kernel(parts, has_base, coarse_ref, fine_ref, *refs):
    out_ref = refs[-1]
    kept = refs[0].shape[0]
    blocks = []
    for place in range(0, len(refs) - 1 - has_base, parts):
        total = refs[place][...]
        for ref in refs[place + 1 : place + parts]:
            total = total + unpack(ref, kept)
        blocks.append(total)
    cross = jnp.concatenate(blocks, axis=1)
    high = cross.astype(jnp.bfloat16)
    low = (cross - high.astype(jnp.float32)).astype(jnp.bfloat16)
    dims = (((1,), (1,)), ((), ()))
    dot = functools.partial(lax.dot_general, dimension_numbers=dims, preferred_element_type=jnp.float32)
    lags = (dot(fine_ref[...], high) + dot(coarse_ref[...], low)) + dot(coarse_ref[...], high)
    if has_base:
        lags = lags + refs[-2][...]
    out_ref[...] = lags


def lag_sums(tables, blocks, base=None):
    parts = len(blocks[0])
    operands = [part for block in blocks for part in block] + ([] if base is None else [base])
    return pl.pallas_call(
        functools.partial(lag_kernel, parts, int(base is not None)),
        out_shape=jax.ShapeDtypeStruct((2 * HALF_LAG + 1, blocks[0][0].shape[0]), jnp.float32),
        compiler_params=params(),
    )(*tables, *operands)


def lag_tables(freq_bins, blocks, scale):
    lags = np.arange(2 * HALF_LAG + 1)[:, None] - HALF_LAG
    columns = []
    for block in blocks:
        bins = np.arange(block * LANES, (block + 1) * LANES)[None, :]
        angles = (bins * lags % (2 * freq_bins)) * (np.pi / freq_bins)
        columns += [np.cos(angles), -np.sin(angles)]
    table = (np.concatenate(columns, axis=1) * scale).astype(np.float32)
    coarse = table.astype(jnp.bfloat16)
    fine = (table - coarse.astype(np.float32)).astype(jnp.bfloat16)
    return jnp.asarray(coarse), jnp.asarray(fine)


def per_device(spectra, send_list, pair_first, pair_second):
    stations, days, segs, width = spectra.shape
    members = lax.axis_size("day")
    tiles = lax.axis_size("tile")
    me = lax.axis_index("day")
    tile = lax.axis_index("tile")
    groups = days * segs
    pairs = pair_first.shape[0]
    kept = pairs // members
    flat = jnp.transpose(spectra, (1, 2, 0, 3)).reshape(groups, stations, width)

    middle, last = tiles // 2, tiles - 1

    def shift(ahead):
        source, target, end = (middle - 1, middle, 0) if ahead else (middle, middle - 1, last)
        pairs = []
        for d in range(members):
            straight = (d >= members // 2) == ahead
            pairs.append((source * members + d, (target if straight else end) * members + d))
            for t in range(tiles - 1):
                if t + 1 != middle:
                    low, high = t * members + d, (t + 1) * members + d
                    pairs.append((low, high) if ahead else (high, low))
        return pairs

    upward, downward = shift(True), shift(False)
    onward = [(d, middle * members + d) for d in range(members // 2)]
    onward += [(last * members + d, (middle - 1) * members + d) for d in range(members // 2, members)]
    both = ("tile", "day")
    side = jnp.where((tile == middle) & (me < members // 2), 1, 0)
    side = jnp.where((tile == middle - 1) & (me >= members // 2), 2, side)
    side = jnp.where(tile == last, 3, side)
    flags = side.astype(jnp.int32).reshape(1)

    def swap(k):
        return [(i, i ^ k) for i in range(members)]

    sent = []
    for chunk in CHUNKS:
        to_below, to_above, flags = lent_rows(flags, flat, send_list, chunk)
        sent.append((lax.ppermute(to_above, both, upward), lax.ppermute(to_below, both, downward)))

    half = members // 2
    order = jnp.stack([me ^ (2 * k + 1) for k in range(half)] + [me ^ (2 * k) for k in range(half)])
    first_ids = pair_first.reshape(members, kept)[order].reshape(pairs, 1)
    second_ids = pair_second.reshape(members, kept)[order].reshape(pairs, 1)

    token = flags
    packed = []
    for chunk, (below, above) in zip(CHUNKS, sent):
        relay = lax.ppermute(jnp.where(flags[0] == 3, above, below), both, onward)
        halo = (below, above, relay)
        send, keep = pair_cross(flags, first_ids, second_ids, flat, halo, chunk, token)
        other = lax.ppermute(send, "day", swap(1))
        pieces = pack(keep, other, keep, half)
        packed.append(
            [pieces[0]]
            + [lax.ppermute(piece, "day", swap(2 * k)) for k, piece in enumerate(pieces) if k]
        )
        token = pieces[0]

    scale = 1.0 / np.sqrt(width * segs * days * members)
    early = [block for chunk in CHUNKS[:-1] for block in chunk]
    lags = lag_sums(lag_tables(width // 2, early, scale), packed[:-1])
    lags = lag_sums(lag_tables(width // 2, CHUNKS[-1], scale), packed[-1:], lags)
    return lags.T


def solution(mesh):
    placed = (P("tile", "day", None, None), P("tile"), P("tile"), P("tile"))
    return jax.shard_map(
        per_device, mesh=mesh, in_specs=placed, out_specs=P(("tile", "day"), None), check_vma=False
    )
```

```python
import functools

import jax
import jax.numpy as jnp
import numpy as np
from jax import lax
from jax.experimental import pallas as pl
from jax.experimental.pallas import tpu as pltpu
from jax.sharding import PartitionSpec as P

HALF_LAG = 500
LANES = 128
CHUNKS = ((0, 1), (2, 3))
PIECE = 32
SEG_STEP = 9
VMEM = 60 << 20
SCALE_ROWS = 16
TOP = 32000.0


def one_hot(ids, width, base):
    slots = lax.broadcasted_iota(jnp.int32, (ids.shape[0], width), 1) + base
    return (ids == slots).astype(jnp.float32).astype(jnp.bfloat16)


def anywhere():
    return pl.BlockSpec(memory_space=pl.ANY)


def scalars():
    return pl.BlockSpec(memory_space=pltpu.SMEM)


def params():
    return pltpu.CompilerParams(vmem_limit_bytes=VMEM)


def border_kernel(flag_ref, send_ref, real_ref, imag_ref, below_ref, above_ref, next_ref, pick_ref):
    next_ref[0] = flag_ref[0]
    next_ref[1] = flag_ref[1]

    @pl.when((pl.program_id(0) == 0) & (pl.program_id(1) == 0))
    def _():
        pick_ref[...] = one_hot(send_ref[...], pick_ref.shape[1], 0)

    half = below_ref.shape[1]
    step = real_ref.shape[0]
    for seg in range(step):
        rows = jnp.concatenate([real_ref[seg], imag_ref[seg]], axis=1)
        lent = jnp.dot(pick_ref[...], rows, preferred_element_type=jnp.float32)
        lent = lent.astype(jnp.bfloat16)
        below_ref[seg] = lent[:half]
        above_ref[seg] = lent[half:]


def lent_rows(flags, spectra, send_list, chunk):
    groups, stations, width = spectra.shape
    count = send_list.shape[0]
    half = count // 2
    first, blocks = chunk[0], len(chunk)
    offset = width // 2 // LANES
    step = 9
    lanes = 2 * LANES * blocks
    out = jax.ShapeDtypeStruct((groups, half, lanes), jnp.bfloat16)
    out_spec = pl.BlockSpec((step, half, 2 * LANES), lambda j, g: (g, 0, j))
    return pl.pallas_call(
        border_kernel,
        grid=(blocks, groups // step),
        in_specs=[
            scalars(),
            pl.BlockSpec((count, 1), lambda j, g: (0, 0)),
            pl.BlockSpec((step, stations, LANES), lambda j, g: (g, 0, first + j)),
            pl.BlockSpec((step, stations, LANES), lambda j, g: (g, 0, first + j + offset)),
        ],
        out_specs=[out_spec, out_spec, scalars()],
        out_shape=[out, out, jax.ShapeDtypeStruct((2,), jnp.int32)],
        scratch_shapes=[pltpu.VMEM((count, stations), jnp.bfloat16)],
        compiler_params=params(),
    )(flags, send_list.reshape(count, 1), spectra, spectra)


def prepare_kernel(
    flag_ref, first_ref, second_ref, own_ref, halo_ref, sort_ref, kind_ref, next_ref, place_ref
):
    next_ref[0] = flag_ref[0]
    next_ref[1] = flag_ref[1]
    me = flag_ref[1]
    members, kept = first_ref.shape
    stations = own_ref.shape[2]
    size = halo_ref.shape[1]

    needs = second_ref[...] >= stations
    marks = needs.astype(jnp.float32)
    rows = lax.broadcasted_iota(jnp.int32, (kept, kept), 0)
    columns = lax.broadcasted_iota(jnp.int32, (kept, kept), 1)
    earlier = (rows < columns).astype(jnp.float32).astype(jnp.bfloat16)
    before = jnp.dot(marks.astype(jnp.bfloat16), earlier, preferred_element_type=jnp.float32)
    count = jnp.sum(marks, axis=1, keepdims=True)
    position = lax.broadcasted_iota(jnp.int32, (members, kept), 1).astype(jnp.float32)
    place = jnp.where(needs, before, count + position - before)
    place_ref[...] = place.astype(jnp.int32)
    most, least = jnp.max(count), jnp.min(count)
    pieces = own_ref.shape[0]
    for piece in range(pieces):
        kind_ref[piece] = (most > piece * PIECE).astype(jnp.int32)
        kind_ref[pieces + piece] = (least < (piece + 1) * PIECE).astype(jnp.int32)

    def choose(ids, width, base):
        slots = lax.broadcasted_iota(jnp.int32, (width, kept), 0) + base
        return (ids == slots).astype(jnp.float32).astype(jnp.bfloat16)

    dims = (((1,), (1,)), ((), ()))
    for slot in range(members):
        half = members // 2
        block = me ^ (2 * slot + 1 if slot < half else 2 * (slot - half))
        row = pl.ds(block, 1)
        sort = choose(place_ref[row, :], kept, 0)
        if slot == half:
            sort_ref[...] = sort
        first, second = first_ref[row, :], second_ref[row, :]
        picks = [choose(first, stations, 0), choose(second, stations, 0), choose(second, halo_ref.shape[2], stations)]
        a, b, c = [
            lax.dot_general(sort, pick, dims, preferred_element_type=jnp.float32).astype(jnp.bfloat16)
            for pick in picks
        ]
        for piece in range(pieces):
            part = slice(piece * PIECE, (piece + 1) * PIECE)
            start = slot * PIECE
            own_ref[piece, start : start + PIECE] = a[part]
            own_ref[piece, size + start : size + start + PIECE] = b[part]
            halo_ref[piece, start : start + PIECE] = c[part]


def prepare(flags, first_ids, second_ids, stations, lent):
    members, kept = first_ids.shape
    pieces, size = kept // PIECE, members * PIECE
    whole = pl.BlockSpec(memory_space=pltpu.VMEM)
    return pl.pallas_call(
        prepare_kernel,
        in_specs=[scalars(), whole, whole],
        out_specs=[whole, whole, whole, scalars(), scalars()],
        out_shape=[
            jax.ShapeDtypeStruct((pieces, 2 * size, stations), jnp.bfloat16),
            jax.ShapeDtypeStruct((pieces, size, 2 * lent), jnp.bfloat16),
            jax.ShapeDtypeStruct((kept, kept), jnp.bfloat16),
            jax.ShapeDtypeStruct((2 * pieces,), jnp.int32),
            jax.ShapeDtypeStruct((2,), jnp.int32),
        ],
        scratch_shapes=[pltpu.VMEM((members, kept), jnp.int32)],
        compiler_params=params(),
    )(flags, first_ids, second_ids)


def add_products(a, b, sums):
    ar, ai, br, bi = a[:, :LANES], a[:, LANES:], b[:, :LANES], b[:, LANES:]
    real, imag = sums
    return real + (ar * br + ai * bi), imag + (ai * br - ar * bi)


def spots(out_refs, kept, piece):
    return [
        (ref, slice(start + piece * PIECE, start + (piece + 1) * PIECE))
        for ref in out_refs
        for start in range(0, ref.shape[0], kept)
    ]


def read_sums(out_refs, kept, piece):
    rows = jnp.concatenate([ref[part] for ref, part in spots(out_refs, kept, piece)], axis=0)
    return rows[:, :LANES], rows[:, LANES:]


def write_sums(out_refs, kept, piece, sums):
    rows = jnp.concatenate(sums, axis=1)
    for place, (ref, part) in enumerate(spots(out_refs, kept, piece)):
        ref[part] = rows[place * PIECE : (place + 1) * PIECE]


def own_kernel(flag_ref, kind_ref, own_ref, real_ref, imag_ref, send_ref, keep_ref, next_ref):
    next_ref[0] = flag_ref[0]
    next_ref[1] = flag_ref[1]
    pieces = own_ref.shape[0]
    size = own_ref.shape[1] // 2
    kept = pieces * PIECE
    outs = (send_ref, keep_ref)

    @pl.when(pl.program_id(1) == 0)
    def _():
        send_ref[...] = jnp.zeros_like(send_ref)
        keep_ref[...] = jnp.zeros_like(keep_ref)

    for piece in range(pieces):

        @pl.when(kind_ref[piece] == 0)
        def _():
            sums = read_sums(outs, kept, piece)
            for seg in range(real_ref.shape[0]):
                table = jnp.concatenate([real_ref[seg], imag_ref[seg]], axis=1)
                both = jnp.dot(own_ref[piece], table, preferred_element_type=jnp.float32)
                sums = add_products(both[:size], both[size:], sums)
            write_sums(outs, kept, piece, sums)


def own_cross(flags, kinds, own, spectra, pairs):
    groups, stations, width = spectra.shape
    blocks = width // 2 // LANES
    out = jax.ShapeDtypeStruct((pairs // 2, width), jnp.float32)
    return pl.pallas_call(
        own_kernel,
        grid=(blocks, groups // SEG_STEP),
        in_specs=[
            scalars(),
            scalars(),
            pl.BlockSpec(own.shape, lambda j, g: (0, 0, 0)),
            pl.BlockSpec((SEG_STEP, stations, LANES), lambda j, g: (g, 0, j)),
            pl.BlockSpec((SEG_STEP, stations, LANES), lambda j, g: (g, 0, j + blocks)),
        ],
        out_specs=[pl.BlockSpec((pairs // 2, 2 * LANES), lambda j, g: (0, j))] * 2 + [scalars()],
        out_shape=[out, out, jax.ShapeDtypeStruct((2,), jnp.int32)],
        compiler_params=params(),
    )(flags, kinds, own, spectra, spectra)


def cross_kernel(
    flag_ref, kind_ref, own_ref, halo_ref, real_ref, imag_ref, first_send_ref, first_keep_ref,
    below_ref, above_ref, relay_ref, token_ref, near_ref, far_ref, keep_ref, border_ref,
):
    lent = below_ref.shape[1]
    pieces, size = halo_ref.shape[:2]
    kept = pieces * PIECE
    groups = real_ref.shape[0]
    outs = (near_ref, far_ref, keep_ref)
    cut = near_ref.shape[0]

    @pl.when(pl.program_id(1) == 0)
    def _():
        near_ref[...] = first_send_ref[:cut]
        far_ref[...] = first_send_ref[cut:]
        keep_ref[...] = first_keep_ref[...]

    border_ref[:, :lent] = below_ref[...]
    border_ref[:, lent:] = above_ref[...]

    @pl.when(flag_ref[0] == 1)
    def _():
        border_ref[:, :lent] = relay_ref[...]

    @pl.when(flag_ref[0] == 2)
    def _():
        border_ref[:, lent:] = relay_ref[...]

    def add(piece, mixed):
        sums = read_sums(outs, kept, piece)
        for seg in range(groups):
            table = jnp.concatenate([real_ref[seg], imag_ref[seg]], axis=1)
            rows = own_ref[piece] if mixed else own_ref[piece, :size]
            gathered = jnp.dot(rows, table, preferred_element_type=jnp.float32)
            b = jnp.dot(halo_ref[piece], border_ref[seg], preferred_element_type=jnp.float32)
            if mixed:
                b = b + gathered[size:]
            sums = add_products(gathered[:size], b, sums)
        write_sums(outs, kept, piece, sums)

    for piece in range(pieces):
        needed, mixed = kind_ref[piece] == 1, kind_ref[pieces + piece] == 1

        @pl.when(needed & mixed)
        def _():
            add(piece, True)

        @pl.when(needed & jnp.logical_not(mixed))
        def _():
            add(piece, False)


def pair_cross(flags, kinds, own, picks, spectra, firsts, halo, chunk, token):
    groups, stations, width = spectra.shape
    lent = halo[0].shape[1]
    half_pairs = firsts[0].shape[0]
    offset = width // 2 // LANES
    first, parts = chunk[0], len(chunk)
    halo_spec = pl.BlockSpec((SEG_STEP, lent, 2 * LANES), lambda j, g: (g, 0, j))
    first_spec = pl.BlockSpec((half_pairs, 2 * LANES), lambda j, g: (0, first + j))
    heights = (half_pairs // 2, half_pairs // 2, half_pairs)
    return pl.pallas_call(
        cross_kernel,
        grid=(parts, groups // SEG_STEP),
        in_specs=[
            scalars(),
            scalars(),
            pl.BlockSpec(own.shape, lambda j, g: (0, 0, 0)),
            pl.BlockSpec(picks.shape, lambda j, g: (0, 0, 0)),
            pl.BlockSpec((SEG_STEP, stations, LANES), lambda j, g: (g, 0, first + j)),
            pl.BlockSpec((SEG_STEP, stations, LANES), lambda j, g: (g, 0, first + j + offset)),
            first_spec,
            first_spec,
            halo_spec,
            halo_spec,
            halo_spec,
            anywhere(),
        ],
        out_specs=[pl.BlockSpec((height, 2 * LANES), lambda j, g: (0, j)) for height in heights],
        out_shape=[jax.ShapeDtypeStruct((height, 2 * LANES * parts), jnp.float32) for height in heights],
        scratch_shapes=[pltpu.VMEM((SEG_STEP, 2 * lent, 2 * LANES), jnp.bfloat16)],
        compiler_params=params(),
    )(flags, kinds, own, picks, spectra, spectra, *firsts, *halo, token)


def pack_kernel(keep_ref, near_ref, far_ref, token_ref, own_ref, *out_refs):
    kept = own_ref.shape[0]
    cut = near_ref.shape[0]
    own_ref[...] = keep_ref[:kept] + near_ref[:kept]
    for k, out_ref in enumerate(out_refs, 1):
        rows = slice(k * kept, (k + 1) * kept)
        other = near_ref[rows] if rows.stop <= cut else far_ref[rows.start - cut : rows.stop - cut]
        total = keep_ref[rows] + other
        peak = jnp.max(jnp.abs(total), axis=0, keepdims=True)
        power = jnp.ceil(jnp.log2(jnp.maximum(peak, 1e-36) * 1.0001))
        scaled = jnp.round(total * jnp.exp2(-power) * TOP)
        out_ref[:kept] = scaled.astype(jnp.int32).astype(jnp.int16)
        powers = jnp.broadcast_to(power, (SCALE_ROWS, power.shape[1]))
        out_ref[kept:] = powers.astype(jnp.int32).astype(jnp.int16)


def pack(keep, near, far, token, parts):
    rows, lanes = keep.shape
    kept = rows // parts
    coded = jax.ShapeDtypeStruct((kept + SCALE_ROWS, lanes), jnp.int16)
    whole = pl.BlockSpec(memory_space=pltpu.VMEM)
    return pl.pallas_call(
        pack_kernel,
        in_specs=[whole, whole, whole, anywhere()],
        out_specs=[whole] * parts,
        out_shape=[jax.ShapeDtypeStruct((kept, lanes), jnp.float32)] + [coded] * (parts - 1),
        compiler_params=params(),
        cost_estimate=pl.CostEstimate(flops=1, bytes_accessed=1, transcendentals=0),
    )(keep, near, far, token)


def unpack(ref, kept):
    power = ref[kept:].astype(jnp.int32).astype(jnp.float32)[:1]
    return ref[:kept].astype(jnp.int32).astype(jnp.float32) * (1.0 / TOP) * jnp.exp2(power)


def lag_kernel(parts, has_base, coarse_ref, fine_ref, sort_ref, *refs):
    out_ref = refs[-1]
    kept = refs[0].shape[0]
    cross = refs[0][...]
    for ref in refs[1:parts]:
        cross = cross + unpack(ref, kept)

    def dot(left, right, axis):
        dims = (((axis,), (axis,)), ((), ()))
        return lax.dot_general(left, right, dims, preferred_element_type=jnp.float32)

    high = cross.astype(jnp.bfloat16)
    low = (cross - high.astype(jnp.float32)).astype(jnp.bfloat16)
    high = dot(sort_ref[...], high, 0).astype(jnp.bfloat16)
    low = dot(sort_ref[...], low, 0).astype(jnp.bfloat16)
    coarse = coarse_ref[...]
    lags = (dot(fine_ref[...], high, 1) + dot(coarse, low, 1)) + dot(coarse, high, 1)
    if has_base:
        lags = lags + refs[parts][...]
    out_ref[...] = lags


def lag_sums(tables, sort, total, base, token):
    operands = [*tables, sort, *total] + ([] if base is None else [base])
    specs = [pl.BlockSpec(memory_space=pltpu.VMEM)] * len(operands)
    if token is not None:
        operands.append(token)
        specs.append(anywhere())
    return pl.pallas_call(
        functools.partial(lag_kernel, len(total), int(base is not None)),
        in_specs=specs,
        out_shape=jax.ShapeDtypeStruct((2 * HALF_LAG + 1, total[0].shape[0]), jnp.float32),
        compiler_params=params(),
        cost_estimate=pl.CostEstimate(flops=10**11, bytes_accessed=10**9, transcendentals=0),
    )(*operands)


def lag_tables(freq_bins, blocks, scale):
    lags = np.arange(2 * HALF_LAG + 1)[:, None] - HALF_LAG
    columns = []
    for block in blocks:
        bins = np.arange(block * LANES, (block + 1) * LANES)[None, :]
        angles = (bins * lags % (2 * freq_bins)) * (np.pi / freq_bins)
        columns += [np.cos(angles), -np.sin(angles)]
    table = (np.concatenate(columns, axis=1) * scale).astype(np.float32)
    coarse = table.astype(jnp.bfloat16)
    fine = (table - coarse.astype(np.float32)).astype(jnp.bfloat16)
    return jnp.asarray(coarse), jnp.asarray(fine)


def per_device(spectra, send_list, pair_first, pair_second):
    stations, days, segs, width = spectra.shape
    members = lax.axis_size("day")
    tiles = lax.axis_size("tile")
    me = lax.axis_index("day")
    tile = lax.axis_index("tile")
    groups = days * segs
    pairs = pair_first.shape[0]
    kept = pairs // members
    flat = jnp.transpose(spectra, (1, 2, 0, 3)).reshape(groups, stations, width)

    middle, last = tiles // 2, tiles - 1

    def shift(ahead):
        source, target, end = (middle - 1, middle, 0) if ahead else (middle, middle - 1, last)
        pairs = []
        for d in range(members):
            straight = (d >= members // 2) == ahead
            pairs.append((source * members + d, (target if straight else end) * members + d))
            for t in range(tiles - 1):
                if t + 1 != middle:
                    low, high = t * members + d, (t + 1) * members + d
                    pairs.append((low, high) if ahead else (high, low))
        return pairs

    upward, downward = shift(True), shift(False)
    onward = [(d, middle * members + d) for d in range(members // 2)]
    onward += [(last * members + d, (middle - 1) * members + d) for d in range(members // 2, members)]
    both = ("tile", "day")
    side = jnp.where((tile == middle) & (me < members // 2), 1, 0)
    side = jnp.where((tile == middle - 1) & (me >= members // 2), 2, side)
    side = jnp.where(tile == last, 3, side)
    flags = jnp.stack([side.astype(jnp.int32), me.astype(jnp.int32)])

    def swap(k):
        return [(i, i ^ k) for i in range(members)]

    sent = []
    for chunk in CHUNKS:
        to_below, to_above, flags = lent_rows(flags, flat, send_list, chunk)
        sent.append((lax.ppermute(to_above, both, upward), lax.ppermute(to_below, both, downward)))

    half = members // 2
    shape = (members, kept)
    own, picks, sort, kinds, flags = prepare(
        flags, pair_first.reshape(shape), pair_second.reshape(shape), stations, send_list.shape[0] // 2
    )
    *firsts, after_own = own_cross(flags, kinds, own, flat, pairs)

    scale = 1.0 / np.sqrt(width * segs * days * members)
    lags = waiting = None
    gates = [flags] + [after_own] * (len(sent) - 1)
    passing = [
        jnp.where(gate[0] == 3, above, below) for gate, (below, above) in zip(gates, sent)
    ]
    token = passing[-1]
    for chunk, (below, above), passed in zip(CHUNKS, sent, passing):
        halo = (below, above, lax.ppermute(passed, both, onward))
        near, far, keep = pair_cross(flags, kinds, own, picks, flat, firsts, halo, chunk, token)
        near, far = (lax.ppermute(part, "day", swap(1)) for part in (near, far))
        if waiting is not None:
            lags = lag_sums(*waiting, lags, keep)
        pieces = pack(keep, near, far, keep if lags is None else lags, half)
        token = pieces[0]
        total = [pieces[0]] + [
            lax.ppermute(piece, "day", swap(2 * k)) for k, piece in enumerate(pieces) if k
        ]
        waiting = (lag_tables(width // 2, chunk, scale), sort, total)
    lags = lag_sums(*waiting, lags, None)
    return lags.T


def solution(mesh):
    placed = (P("tile", "day", None, None), P("tile"), P("tile"), P("tile"))
    return jax.shard_map(
        per_device, mesh=mesh, in_specs=placed, out_specs=P(("tile", "day"), None), check_vma=False
    )
```

```python
import functools

import jax
import jax.numpy as jnp
import numpy as np
from jax import lax
from jax.experimental import pallas as pl
from jax.experimental.pallas import tpu as pltpu
from jax.sharding import PartitionSpec as P

HALF_LAG = 500
LANES = 128
CHUNKS = ((0, 1), (2, 3))
PIECE = 32
SEG_STEP = 9
VMEM = 60 << 20
SCALE_ROWS = 16
TOP = 32000.0


def anywhere():
    return pl.BlockSpec(memory_space=pl.ANY)


def scalars():
    return pl.BlockSpec(memory_space=pltpu.SMEM)


def params():
    return pltpu.CompilerParams(vmem_limit_bytes=VMEM)


def border_kernel(flag_ref, send_ref, real_ref, imag_ref, below_ref, above_ref, next_ref, pick_ref):
    next_ref[0] = flag_ref[0]
    next_ref[1] = flag_ref[1]

    @pl.when((pl.program_id(0) == 0) & (pl.program_id(1) == 0))
    def _():
        count, stations = pick_ref.shape
        slots = lax.broadcasted_iota(jnp.int32, (stations, count), 0)
        columns = (send_ref[...] == slots).astype(jnp.float32).astype(jnp.bfloat16)
        down = lax.broadcasted_iota(jnp.int32, (count, count), 0)
        across = lax.broadcasted_iota(jnp.int32, (count, count), 1)
        same = (down == across).astype(jnp.float32).astype(jnp.bfloat16)
        dims = (((1,), (1,)), ((), ()))
        turned = lax.dot_general(same, columns, dims, preferred_element_type=jnp.float32)
        pick_ref[...] = turned.astype(jnp.bfloat16)

    half = below_ref.shape[1]
    step = real_ref.shape[0]
    for seg in range(step):
        rows = jnp.concatenate([real_ref[seg], imag_ref[seg]], axis=1)
        lent = jnp.dot(pick_ref[...], rows, preferred_element_type=jnp.float32)
        lent = lent.astype(jnp.bfloat16)
        below_ref[seg] = lent[:half]
        above_ref[seg] = lent[half:]


def lent_rows(flags, spectra, send_list, chunk):
    groups, stations, width = spectra.shape
    count = send_list.shape[0]
    half = count // 2
    first, blocks = chunk[0], len(chunk)
    offset = width // 2 // LANES
    step = 9
    lanes = 2 * LANES * blocks
    out = jax.ShapeDtypeStruct((groups, half, lanes), jnp.bfloat16)
    out_spec = pl.BlockSpec((step, half, 2 * LANES), lambda j, g: (g, 0, j))
    return pl.pallas_call(
        border_kernel,
        grid=(blocks, groups // step),
        in_specs=[
            scalars(),
            pl.BlockSpec((1, count), lambda j, g: (0, 0)),
            pl.BlockSpec((step, stations, LANES), lambda j, g: (g, 0, first + j)),
            pl.BlockSpec((step, stations, LANES), lambda j, g: (g, 0, first + j + offset)),
        ],
        out_specs=[out_spec, out_spec, scalars()],
        out_shape=[out, out, jax.ShapeDtypeStruct((2,), jnp.int32)],
        scratch_shapes=[pltpu.VMEM((count, stations), jnp.bfloat16)],
        compiler_params=params(),
    )(flags, send_list.reshape(1, count), spectra, spectra)


def prepare_kernel(
    flag_ref, first_ref, second_ref, own_ref, halo_ref, sort_ref, kind_ref, next_ref, place_ref
):
    next_ref[0] = flag_ref[0]
    next_ref[1] = flag_ref[1]
    me = flag_ref[1]
    members, kept = first_ref.shape
    stations = own_ref.shape[2]
    size = halo_ref.shape[1]

    needs = second_ref[...] >= stations
    marks = needs.astype(jnp.float32)
    rows = lax.broadcasted_iota(jnp.int32, (kept, kept), 0)
    columns = lax.broadcasted_iota(jnp.int32, (kept, kept), 1)
    earlier = (rows < columns).astype(jnp.float32).astype(jnp.bfloat16)
    before = jnp.dot(marks.astype(jnp.bfloat16), earlier, preferred_element_type=jnp.float32)
    count = jnp.sum(marks, axis=1, keepdims=True)
    position = lax.broadcasted_iota(jnp.int32, (members, kept), 1).astype(jnp.float32)
    place = jnp.where(needs, before, count + position - before)
    place_ref[...] = place.astype(jnp.int32)
    most, least = jnp.max(count), jnp.min(count)
    pieces = own_ref.shape[0]
    for piece in range(pieces):
        kind_ref[piece] = (most > piece * PIECE).astype(jnp.int32)
        kind_ref[pieces + piece] = (least < (piece + 1) * PIECE).astype(jnp.int32)

    def choose(ids, width, base):
        slots = lax.broadcasted_iota(jnp.int32, (width, kept), 0) + base
        return (ids == slots).astype(jnp.float32).astype(jnp.bfloat16)

    dims = (((1,), (1,)), ((), ()))
    for slot in range(members):
        half = members // 2
        block = me ^ (2 * slot + 1 if slot < half else 2 * (slot - half))
        row = pl.ds(block, 1)
        sort = choose(place_ref[row, :], kept, 0)
        if slot == half:
            sort_ref[...] = sort
        first, second = first_ref[row, :], second_ref[row, :]
        picks = [choose(first, stations, 0), choose(second, stations, 0), choose(second, halo_ref.shape[2], stations)]
        a, b, c = [
            lax.dot_general(sort, pick, dims, preferred_element_type=jnp.float32).astype(jnp.bfloat16)
            for pick in picks
        ]
        for piece in range(pieces):
            part = slice(piece * PIECE, (piece + 1) * PIECE)
            start = slot * PIECE
            own_ref[piece, start : start + PIECE] = a[part]
            own_ref[piece, size + start : size + start + PIECE] = b[part]
            halo_ref[piece, start : start + PIECE] = c[part]


def prepare(flags, first_ids, second_ids, stations, lent):
    members, kept = first_ids.shape
    pieces, size = kept // PIECE, members * PIECE
    whole = pl.BlockSpec(memory_space=pltpu.VMEM)
    return pl.pallas_call(
        prepare_kernel,
        in_specs=[scalars(), whole, whole],
        out_specs=[whole, whole, whole, scalars(), scalars()],
        out_shape=[
            jax.ShapeDtypeStruct((pieces, 2 * size, stations), jnp.bfloat16),
            jax.ShapeDtypeStruct((pieces, size, 2 * lent), jnp.bfloat16),
            jax.ShapeDtypeStruct((kept, kept), jnp.bfloat16),
            jax.ShapeDtypeStruct((2 * pieces,), jnp.int32),
            jax.ShapeDtypeStruct((2,), jnp.int32),
        ],
        scratch_shapes=[pltpu.VMEM((members, kept), jnp.int32)],
        compiler_params=params(),
    )(flags, first_ids, second_ids)


def add_products(a, b, sums):
    ar, ai, br, bi = a[:, :LANES], a[:, LANES:], b[:, :LANES], b[:, LANES:]
    real, imag = sums
    return real + (ar * br + ai * bi), imag + (ai * br - ar * bi)


def spots(out_refs, kept, piece):
    return [
        (ref, slice(start + piece * PIECE, start + (piece + 1) * PIECE))
        for ref in out_refs
        for start in range(0, ref.shape[0], kept)
    ]


def read_sums(out_refs, kept, piece):
    rows = jnp.concatenate([ref[part] for ref, part in spots(out_refs, kept, piece)], axis=0)
    return rows[:, :LANES], rows[:, LANES:]


def write_sums(out_refs, kept, piece, sums):
    rows = jnp.concatenate(sums, axis=1)
    for place, (ref, part) in enumerate(spots(out_refs, kept, piece)):
        ref[part] = rows[place * PIECE : (place + 1) * PIECE]


def own_kernel(flag_ref, kind_ref, own_ref, real_ref, imag_ref, send_ref, keep_ref, next_ref):
    next_ref[0] = flag_ref[0]
    next_ref[1] = flag_ref[1]
    pieces = own_ref.shape[0]
    size = own_ref.shape[1] // 2
    kept = pieces * PIECE
    outs = (send_ref, keep_ref)

    @pl.when(pl.program_id(1) == 0)
    def _():
        send_ref[...] = jnp.zeros_like(send_ref)
        keep_ref[...] = jnp.zeros_like(keep_ref)

    for piece in range(pieces):

        @pl.when(kind_ref[piece] == 0)
        def _():
            sums = read_sums(outs, kept, piece)
            for seg in range(real_ref.shape[0]):
                table = jnp.concatenate([real_ref[seg], imag_ref[seg]], axis=1)
                both = jnp.dot(own_ref[piece], table, preferred_element_type=jnp.float32)
                sums = add_products(both[:size], both[size:], sums)
            write_sums(outs, kept, piece, sums)


def own_cross(flags, kinds, own, spectra, pairs):
    groups, stations, width = spectra.shape
    blocks = width // 2 // LANES
    out = jax.ShapeDtypeStruct((pairs // 2, width), jnp.float32)
    return pl.pallas_call(
        own_kernel,
        grid=(blocks, groups // SEG_STEP),
        in_specs=[
            scalars(),
            scalars(),
            pl.BlockSpec(own.shape, lambda j, g: (0, 0, 0)),
            pl.BlockSpec((SEG_STEP, stations, LANES), lambda j, g: (g, 0, j)),
            pl.BlockSpec((SEG_STEP, stations, LANES), lambda j, g: (g, 0, j + blocks)),
        ],
        out_specs=[pl.BlockSpec((pairs // 2, 2 * LANES), lambda j, g: (0, j))] * 2 + [scalars()],
        out_shape=[out, out, jax.ShapeDtypeStruct((2,), jnp.int32)],
        compiler_params=params(),
    )(flags, kinds, own, spectra, spectra)


def cross_kernel(
    flag_ref, kind_ref, own_ref, halo_ref, real_ref, imag_ref, first_send_ref, first_keep_ref,
    below_ref, above_ref, relay_ref, token_ref, near_ref, far_ref, keep_ref, border_ref,
):
    lent = below_ref.shape[1]
    pieces, size = halo_ref.shape[:2]
    kept = pieces * PIECE
    groups = real_ref.shape[0]
    outs = (near_ref, far_ref, keep_ref)
    cut = near_ref.shape[0]

    @pl.when(pl.program_id(1) == 0)
    def _():
        near_ref[...] = first_send_ref[:cut]
        far_ref[...] = first_send_ref[cut:]
        keep_ref[...] = first_keep_ref[...]

    border_ref[:, :lent] = below_ref[...]
    border_ref[:, lent:] = above_ref[...]

    @pl.when(flag_ref[0] == 1)
    def _():
        border_ref[:, :lent] = relay_ref[...]

    @pl.when(flag_ref[0] == 2)
    def _():
        border_ref[:, lent:] = relay_ref[...]

    def add(piece, mixed):
        sums = read_sums(outs, kept, piece)
        for seg in range(groups):
            table = jnp.concatenate([real_ref[seg], imag_ref[seg]], axis=1)
            rows = own_ref[piece] if mixed else own_ref[piece, :size]
            gathered = jnp.dot(rows, table, preferred_element_type=jnp.float32)
            b = jnp.dot(halo_ref[piece], border_ref[seg], preferred_element_type=jnp.float32)
            if mixed:
                b = b + gathered[size:]
            sums = add_products(gathered[:size], b, sums)
        write_sums(outs, kept, piece, sums)

    for piece in range(pieces):
        needed, mixed = kind_ref[piece] == 1, kind_ref[pieces + piece] == 1

        @pl.when(needed & mixed)
        def _():
            add(piece, True)

        @pl.when(needed & jnp.logical_not(mixed))
        def _():
            add(piece, False)


def pair_cross(flags, kinds, own, picks, spectra, firsts, halo, chunk, token):
    groups, stations, width = spectra.shape
    lent = halo[0].shape[1]
    half_pairs = firsts[0].shape[0]
    offset = width // 2 // LANES
    first, parts = chunk[0], len(chunk)
    halo_spec = pl.BlockSpec((SEG_STEP, lent, 2 * LANES), lambda j, g: (g, 0, j))
    first_spec = pl.BlockSpec((half_pairs, 2 * LANES), lambda j, g: (0, first + j))
    heights = (half_pairs // 2, half_pairs // 2, half_pairs)
    return pl.pallas_call(
        cross_kernel,
        grid=(parts, groups // SEG_STEP),
        in_specs=[
            scalars(),
            scalars(),
            pl.BlockSpec(own.shape, lambda j, g: (0, 0, 0)),
            pl.BlockSpec(picks.shape, lambda j, g: (0, 0, 0)),
            pl.BlockSpec((SEG_STEP, stations, LANES), lambda j, g: (g, 0, first + j)),
            pl.BlockSpec((SEG_STEP, stations, LANES), lambda j, g: (g, 0, first + j + offset)),
            first_spec,
            first_spec,
            halo_spec,
            halo_spec,
            halo_spec,
            anywhere(),
        ],
        out_specs=[pl.BlockSpec((height, 2 * LANES), lambda j, g: (0, j)) for height in heights],
        out_shape=[jax.ShapeDtypeStruct((height, 2 * LANES * parts), jnp.float32) for height in heights],
        scratch_shapes=[pltpu.VMEM((SEG_STEP, 2 * lent, 2 * LANES), jnp.bfloat16)],
        compiler_params=params(),
    )(flags, kinds, own, picks, spectra, spectra, *firsts, *halo, token)


def pack_kernel(keep_ref, near_ref, far_ref, token_ref, own_ref, *out_refs):
    kept = own_ref.shape[0]
    cut = near_ref.shape[0]
    own_ref[...] = keep_ref[:kept] + near_ref[:kept]
    for k, out_ref in enumerate(out_refs, 1):
        rows = slice(k * kept, (k + 1) * kept)
        other = near_ref[rows] if rows.stop <= cut else far_ref[rows.start - cut : rows.stop - cut]
        total = keep_ref[rows] + other
        peak = jnp.max(jnp.abs(total), axis=0, keepdims=True)
        power = jnp.ceil(jnp.log2(jnp.maximum(peak, 1e-36) * 1.0001))
        scaled = jnp.round(total * jnp.exp2(-power) * TOP)
        out_ref[:kept] = scaled.astype(jnp.int32).astype(jnp.int16)
        powers = jnp.broadcast_to(power, (SCALE_ROWS, power.shape[1]))
        out_ref[kept:] = powers.astype(jnp.int32).astype(jnp.int16)


def pack(keep, near, far, token, parts):
    rows, lanes = keep.shape
    kept = rows // parts
    coded = jax.ShapeDtypeStruct((kept + SCALE_ROWS, lanes), jnp.int16)
    whole = pl.BlockSpec(memory_space=pltpu.VMEM)
    return pl.pallas_call(
        pack_kernel,
        in_specs=[whole, whole, whole, anywhere()],
        out_specs=[whole] * parts,
        out_shape=[jax.ShapeDtypeStruct((kept, lanes), jnp.float32)] + [coded] * (parts - 1),
        compiler_params=params(),
        cost_estimate=pl.CostEstimate(flops=1, bytes_accessed=1, transcendentals=0),
    )(keep, near, far, token)


def unpack(ref, kept):
    power = ref[kept:].astype(jnp.int32).astype(jnp.float32)[:1]
    return ref[:kept].astype(jnp.int32).astype(jnp.float32) * (1.0 / TOP) * jnp.exp2(power)


def lag_kernel(parts, has_base, coarse_ref, fine_ref, sort_ref, *refs):
    out_ref = refs[-1]
    kept = refs[0].shape[0]
    cross = refs[0][...]
    for ref in refs[1:parts]:
        cross = cross + unpack(ref, kept)

    def dot(left, right, axis):
        dims = (((axis,), (axis,)), ((), ()))
        return lax.dot_general(left, right, dims, preferred_element_type=jnp.float32)

    high = cross.astype(jnp.bfloat16)
    low = (cross - high.astype(jnp.float32)).astype(jnp.bfloat16)
    high = dot(sort_ref[...], high, 0).astype(jnp.bfloat16)
    low = dot(sort_ref[...], low, 0).astype(jnp.bfloat16)
    coarse = coarse_ref[...]
    lags = (dot(fine_ref[...], high, 1) + dot(coarse, low, 1)) + dot(coarse, high, 1)
    if has_base:
        lags = lags + refs[parts][...]
    out_ref[...] = lags


def lag_sums(tables, sort, total, base, token):
    operands = [*tables, sort, *total] + ([] if base is None else [base])
    specs = [pl.BlockSpec(memory_space=pltpu.VMEM)] * len(operands)
    if token is not None:
        operands.append(token)
        specs.append(anywhere())
    return pl.pallas_call(
        functools.partial(lag_kernel, len(total), int(base is not None)),
        in_specs=specs,
        out_shape=jax.ShapeDtypeStruct((2 * HALF_LAG + 1, total[0].shape[0]), jnp.float32),
        compiler_params=params(),
        cost_estimate=pl.CostEstimate(flops=10**11, bytes_accessed=10**9, transcendentals=0),
    )(*operands)


def lag_tables(freq_bins, blocks, scale):
    lags = np.arange(2 * HALF_LAG + 1)[:, None] - HALF_LAG
    columns = []
    for block in blocks:
        bins = np.arange(block * LANES, (block + 1) * LANES)[None, :]
        angles = (bins * lags % (2 * freq_bins)) * (np.pi / freq_bins)
        columns += [np.cos(angles), -np.sin(angles)]
    table = (np.concatenate(columns, axis=1) * scale).astype(np.float32)
    coarse = table.astype(jnp.bfloat16)
    fine = (table - coarse.astype(np.float32)).astype(jnp.bfloat16)
    return jnp.asarray(coarse), jnp.asarray(fine)


def per_device(spectra, send_list, pair_first, pair_second):
    stations, days, segs, width = spectra.shape
    members = lax.axis_size("day")
    tiles = lax.axis_size("tile")
    me = lax.axis_index("day")
    tile = lax.axis_index("tile")
    groups = days * segs
    pairs = pair_first.shape[0]
    kept = pairs // members
    flat = jnp.transpose(spectra, (1, 2, 0, 3)).reshape(groups, stations, width)

    middle, last = tiles // 2, tiles - 1

    def shift(ahead):
        source, target, end = (middle - 1, middle, 0) if ahead else (middle, middle - 1, last)
        pairs = []
        for d in range(members):
            straight = (d >= members // 2) == ahead
            pairs.append((source * members + d, (target if straight else end) * members + d))
            for t in range(tiles - 1):
                if t + 1 != middle:
                    low, high = t * members + d, (t + 1) * members + d
                    pairs.append((low, high) if ahead else (high, low))
        return pairs

    upward, downward = shift(True), shift(False)
    onward = [(d, middle * members + d) for d in range(members // 2)]
    onward += [(last * members + d, (middle - 1) * members + d) for d in range(members // 2, members)]
    both = ("tile", "day")
    side = jnp.where((tile == middle) & (me < members // 2), 1, 0)
    side = jnp.where((tile == middle - 1) & (me >= members // 2), 2, side)
    side = jnp.where(tile == last, 3, side)
    flags = jnp.stack([side.astype(jnp.int32), me.astype(jnp.int32)])

    def swap(k):
        return [(i, i ^ k) for i in range(members)]

    sent = []
    for chunk in CHUNKS:
        to_below, to_above, flags = lent_rows(flags, flat, send_list, chunk)
        sent.append((lax.ppermute(to_above, both, upward), lax.ppermute(to_below, both, downward)))

    half = members // 2
    shape = (members, kept)
    own, picks, sort, kinds, flags = prepare(
        flags, pair_first.reshape(shape), pair_second.reshape(shape), stations, send_list.shape[0] // 2
    )
    *firsts, after_own = own_cross(flags, kinds, own, flat, pairs)

    scale = 1.0 / np.sqrt(width * segs * days * members)
    lags = waiting = None
    gates = [flags] + [after_own] * (len(sent) - 1)
    passing = [
        jnp.where(gate[0] == 3, above, below) for gate, (below, above) in zip(gates, sent)
    ]
    token = passing[-1]
    for chunk, (below, above), passed in zip(CHUNKS, sent, passing):
        halo = (below, above, lax.ppermute(passed, both, onward))
        near, far, keep = pair_cross(flags, kinds, own, picks, flat, firsts, halo, chunk, token)
        near, far = (lax.ppermute(part, "day", swap(1)) for part in (near, far))
        if waiting is not None:
            lags = lag_sums(*waiting, lags, keep)
        pieces = pack(keep, near, far, keep if lags is None else lags, half)
        token = pieces[0]
        total = [pieces[0]] + [
            lax.ppermute(piece, "day", swap(2 * k)) for k, piece in enumerate(pieces) if k
        ]
        waiting = (lag_tables(width // 2, chunk, scale), sort, total)
    lags = lag_sums(*waiting, lags, None)
    return lags.T


def solution(mesh):
    placed = (P("tile", "day", None, None), P("tile"), P("tile"), P("tile"))
    return jax.shard_map(
        per_device, mesh=mesh, in_specs=placed, out_specs=P(("tile", "day"), None), check_vma=False
    )
```
